32 devices in a mesh: island: 16 (over z, x, core), fsdp: 2 (over y).
Axes of the slice: x: 2, y: 2, z: 4, core: 2. Of those that a mesh axis runs over, the one named last changes fastest.
Arguments:
- hidden: bfloat16 [16, 256, 8192], P('island', 'fsdp'), may hold values from -6 to 6
- gain: bfloat16 [8192], P('fsdp'), may hold values from 0.5 to 1.5
- doc_ids: int32 [16, 256], P('island', 'fsdp'), may hold values from 0 to 7, never falling along the last dimension, each value on 1 to 64 neighbouring positions
- cotangent: bfloat16 [16, 256, 512], P('island', 'fsdp'), may hold values from -0.1796875 to 0.1796875
- pseudo_grad: bfloat16 [16, 8192, 512], P('island', 'fsdp'), may hold values from -0.375 to 0.375
- outer_weight: float32 [8192, 512], P(('fsdp', 'island')), may hold values from -0.0625 to 0.0625
- momentum: float32 [8192, 512], P(('fsdp', 'island')), may hold values from -0.0625 to 0.0625
Outputs:
- keys: bfloat16 [16, 256, 512], P('island', 'fsdp')
- grad_weight: bfloat16 [16, 8192, 512], P('island', 'fsdp')
- grad_gain: float32 [16, 8192], P('island', 'fsdp')
- new_outer: float32 [8192, 512], P(('fsdp', 'island'))
- new_momentum: float32 [8192, 512], P(('fsdp', 'island'))
The draws below stay inside these ranges and needn't reach their ends.
Inputs may be any that keep to these rules, and one draw needn't show every extreme that they name: `doc_ids`: document numbers never fall along a replica's sequence; every document holds 1 to 64 tokens, and one holds exactly 64.
All inputs are finite; a program needn't handle non-finite values.
Results may differ from the reference program's by a relative error of at most 0.014.
Values may be sent and summed in bfloat16 or wider, within the bound.
A program may use at most 128 MiB of HBM per device.

```python
import math
import jax
import jax.numpy as jnp
import numpy as np
from jax import lax

D = 8192
HEAD = 128
TOK_DEV = 128
DOCS = 8
COLS = 512
SEQ = 256
ISLANDS = 16
N_ISLAND = 16
N_FSDP = 2


def spiked(drawn, rng, source, target, shards_of, factor):
    owner, partner = [(jnp.arange(drawn.shape[dim]) // (drawn.shape[dim] // shards_of)).reshape([-1 if axis == dim else 1 for axis in range(drawn.ndim)]) for dim in (source, target)]
    chosen = jax.random.permutation(rng, shards_of)[partner]
    strong = (owner == chosen) | (owner == (partner + shards_of // 2) % shards_of)
    return jnp.where(strong, factor * drawn, drawn)


def level_of(stream_key, shape, shards, smallest, largest):
    factor_of = 1.0
    for dim, parts in shards:
        heights = jax.random.uniform(jax.random.fold_in(jax.random.fold_in(stream_key, 6), dim), (parts,), jnp.float32, smallest / len(shards), largest / len(shards))
        factor_of = factor_of * jnp.repeat(jnp.exp(heights), shape[dim] // parts).reshape((-1,) + (1,) * (len(shape) - 1 - dim))
    return factor_of


def split_up(amount, total, limit, lean):
    weights = [(1 << 20) // math.isqrt(grade ** lean) + 1 for grade in range(2, amount + 1)]
    surplus, counts = total - limit - (amount - 1), [1] * (amount - 1)
    while surplus > 0:
        movable = [i for i in range(amount - 1) if counts[i] < limit]
        mass, remaining = sum([weights[i] for i in movable]), surplus
        for i in movable:
            extra = min(limit - counts[i], max(1, remaining * weights[i] // mass), surplus)
            counts[i] = counts[i] + extra
            surplus = surplus - extra
    return np.array([limit] + counts)


def ragged(stream_key, count, total, limit, slope):
    if count == 2:
        one = jax.random.randint(stream_key, (), max(1, total - limit), min(limit, total - 1) + 1)
        return jnp.stack([one, total - one])
    lengths = jnp.asarray(split_up(count, total, limit, slope), jnp.int32)
    twos = (count - 1) // 2
    donor, sink = lengths[1:1 + 2 * twos:2], lengths[2:2 + 2 * twos:2]
    slack = jnp.minimum(donor - 1, limit - sink)
    shifted = jax.random.randint(jax.random.fold_in(stream_key, 1), (twos,), 0, 1 << 20) % (slack + 1)
    lengths = lengths.at[1:1 + 2 * twos:2].set(donor - shifted).at[2:2 + 2 * twos:2].set(sink + shifted)
    return lengths[jax.random.permutation(jax.random.fold_in(stream_key, 2), count)]


def normal_values(key, extent, scale, limit, pieces=(), kind=jnp.bfloat16):
    result = scale * jax.random.normal(key, extent, jnp.float32)
    if pieces:
        result = result * level_of(key, extent, pieces, -0.22, 0.18)
    return jnp.clip(result, -limit, limit).astype(kind)


def bell_draw_with(own_key, dims, deviation, most, pieces, heavy, kind=jnp.bfloat16):
    array = deviation * jax.random.normal(own_key, dims, jnp.float32)
    if pieces:
        array = array * level_of(own_key, dims, pieces, -0.22, 0.18)
    return jnp.clip(spiked(array, jax.random.fold_in(own_key, 3), *heavy), -most, most).astype(kind)


def setup_inputs(seed: int = 0) -> dict:
    arg_keys = jax.random.split(jax.random.key(seed), 8)
    return {
        "hidden": normal_values(arg_keys[0], (ISLANDS, SEQ, D), 1.0, 6.0, ((0, 16), (1, 2))),
        "gain": jnp.clip(1.0 + 0.1 * jax.random.normal(arg_keys[1], (D,), jnp.float32), 0.5, 1.5).astype(jnp.bfloat16),
        "doc_ids": jax.vmap(lambda own: jnp.searchsorted(jnp.cumsum(ragged(own, DOCS, SEQ, SEQ // 4, 1)), jnp.arange(SEQ), side="right"))(jax.random.split(arg_keys[2], ISLANDS)).reshape((ISLANDS, SEQ)).astype(jnp.int32),
        "cotangent": normal_values(arg_keys[3], (ISLANDS, SEQ, COLS), 0.03, 0.1796875, ((0, 16), (1, 2))),
        "pseudo_grad": bell_draw_with(arg_keys[4], (ISLANDS, D, COLS), (D // 16) ** -0.5, 0.375, ((0, 16), (1, 2)), (0, 1, 16, 2.0)),
        "outer_weight": normal_values(arg_keys[5], (D, COLS), D ** -0.5, 0.0625, ((0, 32),), jnp.float32),
        "momentum": normal_values(arg_keys[6], (D, COLS), D ** -0.5, 0.0625, ((0, 32),), jnp.float32),
    }


learn_rate = 0.7
momentum_rate = 0.9
norm_eps = 1e-05
rope_base = 500000.0
far_index = 1 << 30

def angles_for(positions, head_width):
    half_width = head_width // 2
    frequency = jnp.exp(jnp.arange(half_width, dtype=jnp.float32) * (-2.0 * math.log(rope_base) / head_width))
    phases = positions[:, None] * frequency[None, :]
    return (jnp.cos(phases), jnp.sin(phases))

def rotate(values, cosine, sine_part, sign):
    rows = values.shape[0]
    half_width = cosine.shape[1]
    shaped = values.reshape(rows, -1, 2 * half_width)
    leading = shaped[:, :, :half_width]
    second = shaped[:, :, half_width:]
    cos_b = cosine[:, None, :]
    sin_b = sine_part[:, None, :] * sign
    joined = jnp.concatenate([leading * cos_b - second * sin_b, second * cos_b + leading * sin_b], axis=2)
    return joined.reshape(rows, -1)

def reference(hidden, gain, doc_ids, cotangent, pseudo_grad, outer_weight, momentum):
    mean_delta = lax.optimization_barrier(jnp.sum(pseudo_grad.astype(jnp.float32), axis=0)) / N_ISLAND
    new_momentum = momentum_rate * momentum + mean_delta
    new_outer = outer_weight - learn_rate * (mean_delta + momentum_rate * new_momentum)
    weight = new_outer.astype(jnp.bfloat16)
    gain_f = gain.astype(jnp.float32)

    def replica(items):
        states, doc_row, cot_row = items
        seq_len = states.shape[0]
        indices = jnp.arange(seq_len, dtype=jnp.int32)
        documents = jnp.arange(DOCS, dtype=jnp.int32)
        in_document = doc_row[:, None] == documents[None, :]
        starts = lax.optimization_barrier(jnp.min(jnp.where(in_document, indices[:, None], far_index), axis=0))
        doc_start = lax.optimization_barrier(jnp.sum(jnp.where(in_document, starts[None, :], 0), axis=1))
        positions = (indices - doc_start).astype(jnp.float32)
        cosine, sine_part = angles_for(positions, HEAD)
        hidden_f = states.astype(jnp.float32)
        row_scale = lax.rsqrt(lax.optimization_barrier(jnp.mean(hidden_f * hidden_f, axis=1, keepdims=True)) + norm_eps)
        normed = hidden_f * row_scale
        activations = (normed * gain_f[None, :]).astype(jnp.bfloat16)
        projected = jnp.dot(activations, weight, preferred_element_type=jnp.float32)
        rotated = rotate(projected, cosine, sine_part, 1.0).astype(jnp.bfloat16)
        back_grad = rotate(cot_row.astype(jnp.float32), cosine, sine_part, -1.0).astype(jnp.bfloat16)
        hidden_grad = jnp.dot(back_grad, weight.T, preferred_element_type=jnp.float32)
        grad_gain = lax.optimization_barrier(jnp.sum(hidden_grad * normed, axis=0))
        act_blocks = activations.reshape(N_FSDP, TOK_DEV, D).astype(jnp.float32)
        back_blocks = back_grad.reshape(N_FSDP, TOK_DEV, COLS).astype(jnp.float32)
        block_parts = jnp.einsum('btd,bth->bdh', act_blocks, back_blocks).astype(jnp.bfloat16)
        grad_weight = lax.optimization_barrier(jnp.sum(block_parts.astype(jnp.float32), axis=0)).astype(jnp.bfloat16)
        return (rotated, grad_weight, grad_gain)
    keys, grad_weight, grad_gain = lax.map(replica, (hidden, doc_ids, cotangent))
    return (keys, grad_weight, grad_gain, new_outer, new_momentum)
```

```python
import functools
import math

import jax
import jax.numpy as jnp
from jax import lax
from jax.experimental import pallas as pl
from jax.experimental.pallas import tpu as pltpu
from jax.sharding import PartitionSpec as P

HEAD = 128
DOCS = 8


learn_rate = 0.7
momentum_rate = 0.9
norm_eps = 1e-05
rope_base = 500000.0
far_index = 1 << 30


def angles_for(positions, head_width):
    half_width = head_width // 2
    frequency = jnp.exp(
        jnp.arange(half_width, dtype=jnp.float32) * (-2.0 * math.log(rope_base) / head_width)
    )
    phases = positions[:, None] * frequency[None, :]
    return (jnp.cos(phases), jnp.sin(phases))


def rotate(values, cosine, sine_part, sign):
    rows = values.shape[0]
    half_width = cosine.shape[1]
    shaped = values.reshape(rows, -1, 2 * half_width)
    leading = shaped[:, :, :half_width]
    second = shaped[:, :, half_width:]
    cos_b = cosine[:, None, :]
    sin_b = sine_part[:, None, :] * sign
    joined = jnp.concatenate(
        [leading * cos_b - second * sin_b, second * cos_b + leading * sin_b], axis=2
    )
    return joined.reshape(rows, -1)


def exchange_kernel(islands, ways, stages, chunks, *refs):
    (delta, outer, mom, hidden, cot, scale, docs) = refs[:7]
    (weight, new_outer, new_mom, cols, all_cot, all_scale, all_docs) = refs[7:14]
    scratch = list(refs[14:])
    recv = [scratch.pop(0) for _ in range(stages)]
    send = [None] + [scratch.pop(0) for _ in range(stages - 1)]
    kept = [None] + [scratch.pop(0) for _ in range(stages - 1)]
    rs_send, rs_recv, ag_send, ag_recv, f_send, f_recv, local_sem = scratch

    me = lax.axis_index("island")
    way = lax.axis_index("fsdp")
    bits = [me // (1 << k) % 2 for k in range(stages)]
    partners = [me + (1 - 2 * bits[k]) * (1 << k) for k in range(stages)]
    rows = outer.shape[0]
    step = rows // chunks
    width = hidden.shape[1] // ways

    barrier = pltpu.get_barrier_semaphore()
    for k in range(stages):
        pl.semaphore_signal(
            barrier, inc=1, device_id={"island": partners[k]},
            device_id_type=pl.DeviceIdType.MESH,
        )
    for d in range(1, ways):
        pl.semaphore_signal(
            barrier, inc=1, device_id={"fsdp": lax.rem(way + d, ways)},
            device_id_type=pl.DeviceIdType.MESH,
        )
    pl.semaphore_wait(barrier, stages + ways - 1)

    def halving(k, c):
        part = pl.ds(c * step, step)
        src = delta.at[:, 1 - bits[0], part] if k == 0 else send[k].at[:, part]
        return pltpu.make_async_remote_copy(
            src_ref=src, dst_ref=recv[k].at[:, part],
            send_sem=rs_send.at[k, c], recv_sem=rs_recv.at[k, c],
            device_id={"island": partners[k]}, device_id_type=pl.DeviceIdType.MESH,
        )

    def doubling(k, c):
        part = pl.ds(c * step, step)
        span = 1 << (k + 1)
        low = lax.rem(me, span)
        copies = []
        for j in range(islands // span):
            slot = islands - islands // (1 << k) + j
            copies.append(pltpu.make_async_remote_copy(
                src_ref=weight.at[j * span + low, part],
                dst_ref=weight.at[j * span + low, part],
                send_sem=ag_send.at[c, slot], recv_sem=ag_recv.at[c, slot],
                device_id={"island": partners[k]}, device_id_type=pl.DeviceIdType.MESH,
            ))
        return copies

    for c in range(chunks):
        halving(0, c).start()

    pieces = ((cols, None), (all_cot, cot), (all_scale, scale), (all_docs, docs))

    def across(d):
        to = lax.rem(way + d, ways)
        copies = []
        for i, (dst, src) in enumerate(pieces):
            if src is None:
                src = hidden.at[:, pl.ds(pl.multiple_of(to * width, width), width)]
            copies.append(pltpu.make_async_remote_copy(
                src_ref=src, dst_ref=dst.at[way],
                send_sem=f_send.at[d - 1, i], recv_sem=f_recv.at[d - 1, i],
                device_id={"fsdp": to}, device_id_type=pl.DeviceIdType.MESH,
            ))
        return copies

    for d in range(1, ways):
        for copy in across(d):
            copy.start()
    own = []
    for i, (dst, src) in enumerate(pieces):
        if src is None:
            src = hidden.at[:, pl.ds(pl.multiple_of(way * width, width), width)]
        own.append(pltpu.make_async_copy(src, dst.at[way], local_sem.at[i]))
    for copy in own:
        copy.start()

    def reduce_stage(k, c):
        part = pl.ds(c * step, step)
        halving(k, c).wait_recv()

        def total(m):
            mine = delta[m, bits[0], part] if k == 0 else kept[k][m, part]
            return mine.astype(jnp.float32) + recv[k][m, part].astype(jnp.float32)

        if k < stages - 1:
            count = islands >> (k + 2)

            def to_send(j, carry):
                send[k + 1][j, part] = total(2 * j + 1 - bits[k + 1]).astype(jnp.bfloat16)
                return carry

            def to_keep(j, carry):
                kept[k + 1][j, part] = total(2 * j + bits[k + 1])
                return carry

            lax.fori_loop(0, count, to_send, 0)
            halving(k + 1, c).start()
            lax.fori_loop(0, count, to_keep, 0)
        else:
            mean_delta = total(0) / islands
            fresh_mom = momentum_rate * mom[part] + mean_delta
            fresh = outer[part] - learn_rate * (mean_delta + momentum_rate * fresh_mom)
            weight[me, part] = fresh.astype(jnp.bfloat16)
            for copy in doubling(stages - 1, c):
                copy.start()
            new_mom[part] = fresh_mom
            new_outer[part] = fresh

    def gather_stage(k, c):
        for copy in doubling(k, c):
            copy.wait_recv()
        if k > 0:
            for copy in doubling(k - 1, c):
                copy.start()

    for tick in range(2 * stages + chunks - 1):
        for c in range(chunks):
            k = tick - c
            if 0 <= k < stages:
                reduce_stage(k, c)
            elif stages <= k < 2 * stages:
                gather_stage(2 * stages - 1 - k, c)

    for c in range(chunks):
        for k in range(stages):
            halving(k, c).wait_send()
            for copy in doubling(k, c):
                copy.wait_send()
    for d in range(1, ways):
        for copy in across(d):
            copy.wait()
    for copy in own:
        copy.wait()


def exchange(delta, outer, mom, hidden, cot, scale, docs):
    islands = lax.axis_size("island")
    ways = lax.axis_size("fsdp")
    stages = islands.bit_length() - 1
    rows, width = outer.shape
    chunks = 4 if rows % 64 == 0 else 1
    tok, feats = hidden.shape
    bf, f32 = jnp.bfloat16, jnp.float32
    recv = [pltpu.VMEM((islands >> (k + 1), rows, width), bf) for k in range(stages)]
    send = [pltpu.VMEM((islands >> (k + 1), rows, width), bf) for k in range(1, stages)]
    kept = [pltpu.VMEM((islands >> (k + 1), rows, width), f32) for k in range(1, stages)]
    dma = pltpu.SemaphoreType.DMA
    vmem = pl.BlockSpec(memory_space=pltpu.VMEM)
    return pl.pallas_call(
        functools.partial(exchange_kernel, islands, ways, stages, chunks),
        out_shape=(
            jax.ShapeDtypeStruct((islands, rows, width), bf),
            jax.ShapeDtypeStruct((rows, width), f32),
            jax.ShapeDtypeStruct((rows, width), f32),
            jax.ShapeDtypeStruct((ways, tok, feats // ways), bf),
            jax.ShapeDtypeStruct((ways, tok, width), bf),
            jax.ShapeDtypeStruct((ways,) + scale.shape, f32),
            jax.ShapeDtypeStruct((ways,) + docs.shape, jnp.int32),
        ),
        in_specs=[vmem] * 7,
        out_specs=[vmem] * 7,
        scratch_shapes=recv + send + kept + [
            dma((stages, chunks)), dma((stages, chunks)),
            dma((chunks, islands)), dma((chunks, islands)),
            dma((max(ways - 1, 1), 4)), dma((max(ways - 1, 1), 4)), dma((4,)),
        ],
        compiler_params=pltpu.CompilerParams(
            collective_id=0, has_side_effects=True, vmem_limit_bytes=56 * 1024 * 1024
        ),
    )(delta.reshape(islands // 2, 2, rows, width), outer, mom, hidden, cot, scale, docs)


def body(hidden, gain, doc_ids, cotangent, pseudo_grad, outer_weight, momentum):
    fsdp_ways = lax.axis_size("fsdp")
    tok_rows = hidden.shape[1]
    hidden_f = hidden[0].astype(jnp.float32)
    row_scale = lax.rsqrt(jnp.mean(hidden_f * hidden_f, axis=1, keepdims=True) + norm_eps)
    weight, new_outer, new_momentum, columns, all_cot, all_scales, all_docs = exchange(
        pseudo_grad[0], outer_weight, momentum, hidden[0], cotangent[0],
        jnp.broadcast_to(row_scale, (tok_rows, 128)),
        jnp.broadcast_to(doc_ids, (8, tok_rows)),
    )
    weight = weight.reshape(-1, weight.shape[2])
    seq = fsdp_ways * tok_rows
    docs = all_docs[:, 0, :].reshape(seq)
    indices = jnp.arange(seq, dtype=jnp.int32)
    documents = jnp.arange(DOCS, dtype=jnp.int32)
    in_document = docs[:, None] == documents[None, :]
    starts = jnp.min(jnp.where(in_document, indices[:, None], far_index), axis=0)
    doc_start = jnp.sum(jnp.where(in_document, starts[None, :], 0), axis=1)
    positions = (indices - doc_start).astype(jnp.float32)
    cosine, sine_part = angles_for(positions, HEAD)
    all_back = rotate(
        all_cot.reshape(seq, -1).astype(jnp.float32), cosine, sine_part, -1.0
    ).astype(jnp.bfloat16)
    normed_cols = (
        columns.reshape(seq, -1).astype(jnp.float32) * all_scales[:, :, :1].reshape(seq, 1)
    )
    act_cols = (normed_cols * gain.astype(jnp.float32)[None, :]).astype(jnp.bfloat16)
    partial_proj = jnp.dot(act_cols, weight, preferred_element_type=jnp.float32)
    own = lax.axis_index("fsdp")
    if fsdp_ways == 2:
        other = lax.dynamic_slice_in_dim(partial_proj, (1 - own) * tok_rows, tok_rows, 0)
        mine = lax.dynamic_slice_in_dim(partial_proj, own * tok_rows, tok_rows, 0)
        got = lax.ppermute(other.astype(jnp.bfloat16), "fsdp", [(0, 1), (1, 0)])
        projected = mine + got.astype(jnp.float32)
    else:
        projected = lax.psum_scatter(partial_proj, "fsdp", scatter_dimension=0, tiled=True)
    hidden_grad = lax.dot_general(
        all_back, weight, (((1,), (1,)), ((), ())), preferred_element_type=jnp.float32
    )
    grad_gain = jnp.sum(hidden_grad * normed_cols, axis=0)
    grad_weight = jnp.zeros((act_cols.shape[1], all_back.shape[1]), jnp.float32)
    for block in range(fsdp_ways):
        act_block = act_cols[block * tok_rows : (block + 1) * tok_rows]
        back_block = all_back[block * tok_rows : (block + 1) * tok_rows]
        part = lax.dot_general(
            act_block, back_block, (((0,), (0,)), ((), ())), preferred_element_type=jnp.float32
        )
        grad_weight = grad_weight + part.astype(jnp.bfloat16).astype(jnp.float32)
    cos_own = lax.dynamic_slice_in_dim(cosine, own * tok_rows, tok_rows, 0)
    sin_own = lax.dynamic_slice_in_dim(sine_part, own * tok_rows, tok_rows, 0)
    rotated = rotate(projected, cos_own, sin_own, 1.0).astype(jnp.bfloat16)
    return (
        rotated[None],
        grad_weight.astype(jnp.bfloat16)[None],
        grad_gain[None],
        new_outer,
        new_momentum,
    )


def solution(mesh):
    placed = (
        P("island", "fsdp", None),
        P("fsdp"),
        P("island", "fsdp"),
        P("island", "fsdp", None),
        P("island", "fsdp", None),
        P(("fsdp", "island"), None),
        P(("fsdp", "island"), None),
    )
    return jax.shard_map(
        body,
        mesh=mesh,
        in_specs=placed,
        out_specs=(
            P("island", "fsdp", None),
            P("island", "fsdp", None),
            P("island", "fsdp"),
            P(("fsdp", "island"), None),
            P(("fsdp", "island"), None),
        ),
        check_vma=False,
    )
```

```python
import functools
import math

import jax
import jax.numpy as jnp
from jax import lax
from jax.experimental import pallas as pl
from jax.experimental.pallas import tpu as pltpu
from jax.sharding import PartitionSpec as P

HEAD = 128
DOCS = 8


learn_rate = 0.7
momentum_rate = 0.9
norm_eps = 1e-05
rope_base = 500000.0
far_index = 1 << 30


def turn(values, cosine, sine):
    heads = [values[:, i : i + HEAD] for i in range(0, values.shape[1], HEAD)]
    return jnp.concatenate(
        [head * cosine + pltpu.roll(head, HEAD // 2, 1) * sine for head in heads], axis=1
    )


CHUNKS = 4


def orders_for(stages, chunk):
    return list(range(stages))


def exchange_kernel(islands, ways, stages, chunks, *refs):
    (delta, outer, mom, hidden, cot, docs, gain) = refs[:7]
    (weight, new_outer, new_mom, act, back, keys) = refs[7:13]
    (cols, all_cot, info, all_info, part_out, part_in, angles) = refs[13:20]
    scratch = list(refs[20:])
    recv = [scratch.pop(0) for _ in range(stages)]
    send = [None] + [scratch.pop(0) for _ in range(stages - 1)]
    kept = [None] + [scratch.pop(0) for _ in range(stages - 1)]
    rs_send, rs_recv, ag_send, ag_recv, f_send, f_recv, local_sem, p_send, p_recv = scratch
    tok = cot.shape[0]

    me = lax.axis_index("island")
    way = lax.axis_index("fsdp")
    bits = [me // (1 << k) % 2 for k in range(stages)]
    partners = [me + (1 - 2 * bits[k]) * (1 << k) for k in range(stages)]
    rows = outer.shape[0]
    step = rows // chunks
    width = hidden.shape[1] // ways

    barrier = pltpu.get_barrier_semaphore()
    for k in range(stages):
        pl.semaphore_signal(
            barrier, inc=1, device_id={"island": partners[k]},
            device_id_type=pl.DeviceIdType.MESH,
        )
    for d in range(1, ways):
        pl.semaphore_signal(
            barrier, inc=1, device_id={"fsdp": lax.rem(way + d, ways)},
            device_id_type=pl.DeviceIdType.MESH,
        )
    pl.semaphore_wait(barrier, stages + ways - 1)

    orders = [orders_for(stages, c) for c in range(chunks)]

    def halving(k, c):
        part = pl.ds(c * step, step)
        bit = orders[c][k]
        src = delta.at[:, 1 - bits[0], part] if k == 0 else send[k].at[:, part]
        return pltpu.make_async_remote_copy(
            src_ref=src, dst_ref=recv[k].at[:, part],
            send_sem=rs_send.at[k, c], recv_sem=rs_recv.at[k, c],
            device_id={"island": partners[bit]}, device_id_type=pl.DeviceIdType.MESH,
        )

    def doubling(k, c):
        part = pl.ds(c * step, step)
        bit = orders[c][k]
        fixed = sum(bits[b] * (1 << b) for b in orders[c][: k + 1])
        copies = []
        for j in range(islands >> (k + 1)):
            slot = islands - islands // (1 << k) + j
            block = fixed + sum((j >> i & 1) << b for i, b in enumerate(orders[c][k + 1 :]))
            copies.append(pltpu.make_async_remote_copy(
                src_ref=weight.at[block, part], dst_ref=weight.at[block, part],
                send_sem=ag_send.at[c, slot], recv_sem=ag_recv.at[c, slot],
                device_id={"island": partners[bit]}, device_id_type=pl.DeviceIdType.MESH,
            ))
        return copies

    for c in range(chunks):
        halving(0, c).start()

    pieces = ((cols, None), (all_cot, cot), (all_info, info))

    def across(d):
        to = lax.rem(way + d, ways)
        copies = []
        for i, (dst, src) in enumerate(pieces):
            if src is None:
                src = hidden.at[:, pl.ds(pl.multiple_of(to * width, width), width)]
            copies.append(pltpu.make_async_remote_copy(
                src_ref=src, dst_ref=dst.at[way],
                send_sem=f_send.at[d - 1, i], recv_sem=f_recv.at[d - 1, i],
                device_id={"fsdp": to}, device_id_type=pl.DeviceIdType.MESH,
            ))
        return copies

    for d in range(1, ways):
        for copy in across(d)[:2]:
            copy.start()
    own = []
    for i, (dst, src) in enumerate(pieces):
        if src is None:
            src = hidden.at[:, pl.ds(pl.multiple_of(way * width, width), width)]
        own.append(pltpu.make_async_copy(src, dst.at[way], local_sem.at[i]))
    for copy in own[:2]:
        copy.start()

    tile = 512

    def cut(i):
        return pl.ds(pl.multiple_of(i * tile, tile), tile)

    def norms():
        def add(i, total):
            block = hidden[:, cut(i)].astype(jnp.float32)
            block = block * block
            for lane in range(0, tile, HEAD):
                total = total + block[:, lane : lane + HEAD]
            return total

        squares = lax.fori_loop(
            0, hidden.shape[1] // tile, add, jnp.zeros((tok, HEAD), jnp.float32)
        )
        mean = jnp.sum(squares, axis=1, keepdims=True) / hidden.shape[1]
        info[0] = jnp.broadcast_to(lax.rsqrt(mean + norm_eps), (tok, HEAD))
        row = docs[...].astype(jnp.float32)
        info[1] = jnp.broadcast_to(row, (HEAD, tok)).T
        for d in range(1, ways):
            across(d)[2].start()
        own[2].start()

    def arrivals():
        for d in range(1, ways):
            for copy in across(d):
                copy.wait_recv()
        for copy in own:
            copy.wait()

    def find_angles():
        shape = (tok, HEAD)
        lane = lax.broadcasted_iota(jnp.int32, shape, 1)
        first_half = lane < HEAD // 2
        half_lane = jnp.where(first_half, lane, lane - HEAD // 2).astype(jnp.float32)
        frequency = jnp.exp(half_lane * (-2.0 * math.log(rope_base) / HEAD))
        token = lax.broadcasted_iota(jnp.int32, shape, 0).astype(jnp.float32)
        starts = []
        for s in range(DOCS):
            first = jnp.full((1, HEAD), float(far_index), jnp.float32)
            for f in range(ways):
                at = jnp.where(all_info[f, 1] == float(s), token + f * tok, float(far_index))
                first = jnp.minimum(first, jnp.min(at, axis=0, keepdims=True))
            starts.append(first)
        for f in range(ways):
            start = jnp.zeros(shape, jnp.float32)
            for s in range(DOCS):
                start = start + jnp.where(all_info[f, 1] == float(s), starts[s], 0.0)
            phases = (token + f * tok - start) * frequency
            sine = jnp.sin(phases)
            angles[f, 0] = jnp.cos(phases)
            angles[f, 1] = jnp.where(first_half, sine, -sine)

    def turn_back():
        for f in range(ways):
            back[pl.ds(f * tok, tok)] = turn(
                all_cot[f].astype(jnp.float32), angles[f, 0], angles[f, 1]
            ).astype(jnp.bfloat16)

    def activate(f):
        scale = all_info[f, 0][:, :1]

        def one(i, carry):
            normed = cols[f, :, cut(i)].astype(jnp.float32) * scale
            act[pl.ds(f * tok, tok), cut(i)] = (normed * gain[:, cut(i)]).astype(jnp.bfloat16)
            return carry

        lax.fori_loop(0, width // tile, one, 0)

    work = [arrivals, find_angles, turn_back]
    work += [functools.partial(activate, f) for f in range(ways)]

    def reduce_stage(k, c):
        part = pl.ds(c * step, step)
        halving(k, c).wait_recv()

        def total(m):
            mine = delta[m, bits[0], part] if k == 0 else kept[k][m, part]
            return mine.astype(jnp.float32) + recv[k][m, part].astype(jnp.float32)

        if k < stages - 1:
            count = islands >> (k + 2)
            following = orders[c][k + 1]
            below = 1 << sorted(orders[c][k + 1 :]).index(following)

            def place(j, bit):
                return j // below * (2 * below) + bit * below + j % below

            def to_send(j, carry):
                send[k + 1][j, part] = total(place(j, 1 - bits[following])).astype(jnp.bfloat16)
                return carry

            def to_keep(j, carry):
                kept[k + 1][j, part] = total(place(j, bits[following]))
                return carry

            lax.fori_loop(0, count, to_send, 0)
            halving(k + 1, c).start()
            lax.fori_loop(0, count, to_keep, 0)
        else:
            mean_delta = total(0) / islands
            fresh_mom = momentum_rate * mom[part] + mean_delta
            fresh = outer[part] - learn_rate * (mean_delta + momentum_rate * fresh_mom)
            weight[me, part] = fresh.astype(jnp.bfloat16)
            for copy in doubling(stages - 1, c):
                copy.start()
            new_mom[part] = fresh_mom
            new_outer[part] = fresh

    def gather_stage(k, c):
        for copy in doubling(k, c):
            copy.wait_recv()
        if k > 0:
            for copy in doubling(k - 1, c):
                copy.start()

    for tick in range(2 * stages + chunks - 1):
        for c in range(chunks):
            k = tick - c
            if 0 <= k < stages:
                reduce_stage(k, c)
                if tick == 1 and c == 0:
                    norms()
            elif stages <= k < 2 * stages:
                if work:
                    work.pop(0)()
                gather_stage(2 * stages - 1 - k, c)

    while work:
        work.pop(0)()

    def product(f):
        tokens = act[pl.ds(pl.multiple_of(f * tok, tok), tok), :]
        whole = weight[...].reshape(width, cot.shape[1])
        return jnp.dot(tokens, whole, preferred_element_type=jnp.float32)

    def swap(d):
        return pltpu.make_async_remote_copy(
            src_ref=part_out.at[d - 1], dst_ref=part_in.at[d - 1],
            send_sem=p_send.at[d - 1], recv_sem=p_recv.at[d - 1],
            device_id={"fsdp": lax.rem(way + d, ways)},
            device_id_type=pl.DeviceIdType.MESH,
        )

    for d in range(1, ways):
        part_out[d - 1] = product(lax.rem(way + d, ways)).astype(jnp.bfloat16)
        swap(d).start()
    projected = product(way)
    for c in range(chunks):
        for k in range(stages):
            halving(k, c).wait_send()
            for copy in doubling(k, c):
                copy.wait_send()
    for d in range(1, ways):
        for copy in across(d):
            copy.wait_send()
    for d in range(1, ways):
        swap(d).wait_recv()
        projected = projected + part_in[d - 1].astype(jnp.float32)
    keys[...] = turn(projected, angles[way, 0], -angles[way, 1]).astype(jnp.bfloat16)
    for d in range(1, ways):
        swap(d).wait_send()


def exchange(delta, outer, mom, hidden, cot, docs, gain):
    islands = lax.axis_size("island")
    ways = lax.axis_size("fsdp")
    stages = islands.bit_length() - 1
    rows, width = outer.shape
    chunks = CHUNKS if rows % (16 * CHUNKS) == 0 else 1
    tok, feats = hidden.shape
    bf, f32 = jnp.bfloat16, jnp.float32
    recv = [pltpu.VMEM((islands >> (k + 1), rows, width), bf) for k in range(stages)]
    send = [pltpu.VMEM((islands >> (k + 1), rows, width), bf) for k in range(1, stages)]
    kept = [pltpu.VMEM((islands >> (k + 1), rows, width), f32) for k in range(1, stages)]
    dma = pltpu.SemaphoreType.DMA
    vmem = pl.BlockSpec(memory_space=pltpu.VMEM)
    return pl.pallas_call(
        functools.partial(exchange_kernel, islands, ways, stages, chunks),
        out_shape=(
            jax.ShapeDtypeStruct((islands, rows, width), bf),
            jax.ShapeDtypeStruct((rows, width), f32),
            jax.ShapeDtypeStruct((rows, width), f32),
            jax.ShapeDtypeStruct((ways * tok, feats // ways), bf),
            jax.ShapeDtypeStruct((ways * tok, width), bf),
            jax.ShapeDtypeStruct((tok, width), bf),
        ),
        in_specs=[vmem] * 7,
        out_specs=[vmem] * 6,
        scratch_shapes=[
            pltpu.VMEM((ways, tok, feats // ways), bf),
            pltpu.VMEM((ways, tok, width), bf),
            pltpu.VMEM((2, tok, HEAD), f32),
            pltpu.VMEM((ways, 2, tok, HEAD), f32),
            pltpu.VMEM((max(ways - 1, 1), tok, width), bf),
            pltpu.VMEM((max(ways - 1, 1), tok, width), bf),
            pltpu.VMEM((ways, 2, tok, HEAD), f32),
        ] + recv + send + kept + [
            dma((stages, chunks)), dma((stages, chunks)),
            dma((chunks, islands)), dma((chunks, islands)),
            dma((max(ways - 1, 1), 3)), dma((max(ways - 1, 1), 3)), dma((3,)),
            dma((max(ways - 1, 1),)), dma((max(ways - 1, 1),)),
        ],
        compiler_params=pltpu.CompilerParams(
            collective_id=0, has_side_effects=True, vmem_limit_bytes=56 * 1024 * 1024
        ),
    )(delta.reshape(islands // 2, 2, rows, width), outer, mom, hidden, cot, docs, gain)


def gradient_kernel(act, back, weight, gain, keys, outer, mom, *outs):
    (grad_weight, grad_gain, keys_out, outer_out, mom_out) = outs
    grad = lax.dot_general(
        act[...], back[...], (((0,), (0,)), ((), ())), preferred_element_type=jnp.float32
    )
    grad_weight[...] = grad.astype(jnp.bfloat16)
    ones = jnp.ones((8, grad.shape[1]), jnp.float32)
    sums = lax.dot_general(
        ones, grad * weight[...].astype(jnp.float32), (((1,), (1,)), ((), ())),
        precision=lax.Precision.HIGHEST, preferred_element_type=jnp.float32,
    )
    grad_gain[...] = sums[:1] / gain[...]
    keys_out[...] = keys[...]
    outer_out[...] = outer[...]
    mom_out[...] = mom[...]


def gradients(act, back, weight, gain, keys, outer, mom):
    seq, feats = act.shape
    width = back.shape[1]
    tiles = feats // 512

    def rows_of(array):
        return pl.BlockSpec((array.shape[0] // tiles, width), lambda i: (i, 0))

    row = pl.BlockSpec((1, 512), lambda i: (0, i))
    shape = jax.ShapeDtypeStruct
    return pl.pallas_call(
        gradient_kernel,
        grid=(tiles,),
        in_specs=[
            pl.BlockSpec((seq, 512), lambda i: (0, i)),
            pl.BlockSpec((seq, width), lambda i: (0, 0)),
            rows_of(weight), row, rows_of(keys), rows_of(outer), rows_of(mom),
        ],
        out_specs=[rows_of(weight), row, rows_of(keys), rows_of(outer), rows_of(mom)],
        out_shape=[
            shape(weight.shape, jnp.bfloat16), shape((1, feats), jnp.float32),
            shape(keys.shape, keys.dtype), shape(outer.shape, outer.dtype),
            shape(mom.shape, mom.dtype),
        ],
        compiler_params=pltpu.CompilerParams(vmem_limit_bytes=32 * 1024 * 1024),
    )(act, back, weight, gain, keys, outer, mom)


def body(hidden, gain, doc_ids, cotangent, pseudo_grad, outer_weight, momentum):
    gain_row = gain.astype(jnp.float32)[None, :]
    weight, new_outer, new_momentum, act, back, keys = exchange(
        pseudo_grad[0], outer_weight, momentum, hidden[0], cotangent[0], doc_ids, gain_row
    )
    grad_weight, grad_gain, keys, new_outer, new_momentum = gradients(
        act, back, weight.reshape(-1, weight.shape[2]), gain_row, keys, new_outer, new_momentum
    )
    return keys[None], grad_weight[None], grad_gain, new_outer, new_momentum


def solution(mesh):
    placed = (
        P("island", "fsdp", None),
        P("fsdp"),
        P("island", "fsdp"),
        P("island", "fsdp", None),
        P("island", "fsdp", None),
        P(("fsdp", "island"), None),
        P(("fsdp", "island"), None),
    )
    return jax.shard_map(
        body,
        mesh=mesh,
        in_specs=placed,
        out_specs=(
            P("island", "fsdp", None),
            P("island", "fsdp", None),
            P("island", "fsdp"),
            P(("fsdp", "island"), None),
            P(("fsdp", "island"), None),
        ),
        check_vma=False,
    )
```

```python
import functools
import math

import jax
import jax.numpy as jnp
from jax import lax
from jax.experimental import pallas as pl
from jax.experimental.pallas import tpu as pltpu
from jax.sharding import PartitionSpec as P

HEAD = 128
DOCS = 8


learn_rate = 0.7
momentum_rate = 0.9
norm_eps = 1e-05
rope_base = 500000.0
far_index = 1 << 30


def turn(values, cosine, sine):
    heads = [values[:, i : i + HEAD] for i in range(0, values.shape[1], HEAD)]
    return jnp.concatenate(
        [head * cosine + pltpu.roll(head, HEAD // 2, 1) * sine for head in heads], axis=1
    )


CHUNKS = 4


def orders_for(stages, chunk):
    return list(range(stages))


def exchange_kernel(islands, ways, stages, chunks, *refs):
    (delta, outer, mom, hidden, cot, docs, gain) = refs[:7]
    (weight, new_outer, new_mom, act, back, keys) = refs[7:13]
    (cols, all_cot, info, all_info, part_out, part_in, angles) = refs[13:20]
    scratch = list(refs[20:])
    recv = [scratch.pop(0) for _ in range(stages)]
    send = [None] + [scratch.pop(0) for _ in range(stages - 1)]
    kept = [None] + [scratch.pop(0) for _ in range(stages - 1)]
    rs_send, rs_recv, ag_send, ag_recv, f_send, f_recv, local_sem, p_send, p_recv = scratch
    tok = cot.shape[0]

    me = lax.axis_index("island")
    way = lax.axis_index("fsdp")
    bits = [me // (1 << k) % 2 for k in range(stages)]
    partners = [me + (1 - 2 * bits[k]) * (1 << k) for k in range(stages)]
    rows = outer.shape[0]
    step = rows // chunks
    width = hidden.shape[1] // ways

    barrier = pltpu.get_barrier_semaphore()
    for k in range(stages):
        pl.semaphore_signal(
            barrier, inc=1, device_id={"island": partners[k]},
            device_id_type=pl.DeviceIdType.MESH,
        )
    for d in range(1, ways):
        pl.semaphore_signal(
            barrier, inc=1, device_id={"fsdp": lax.rem(way + d, ways)},
            device_id_type=pl.DeviceIdType.MESH,
        )
    pl.semaphore_wait(barrier, stages + ways - 1)

    orders = [orders_for(stages, c) for c in range(chunks)]

    def halving(k, c):
        part = pl.ds(c * step, step)
        bit = orders[c][k]
        src = delta.at[:, 1 - bits[0], part] if k == 0 else send[k].at[:, part]
        return pltpu.make_async_remote_copy(
            src_ref=src, dst_ref=recv[k].at[:, part],
            send_sem=rs_send.at[k, c], recv_sem=rs_recv.at[k, c],
            device_id={"island": partners[bit]}, device_id_type=pl.DeviceIdType.MESH,
        )

    def doubling(k, c):
        part = pl.ds(c * step, step)
        bit = orders[c][k]
        fixed = sum(bits[b] * (1 << b) for b in orders[c][: k + 1])
        copies = []
        for j in range(islands >> (k + 1)):
            slot = islands - islands // (1 << k) + j
            block = fixed + sum((j >> i & 1) << b for i, b in enumerate(orders[c][k + 1 :]))
            copies.append(pltpu.make_async_remote_copy(
                src_ref=weight.at[block, part], dst_ref=weight.at[block, part],
                send_sem=ag_send.at[c, slot], recv_sem=ag_recv.at[c, slot],
                device_id={"island": partners[bit]}, device_id_type=pl.DeviceIdType.MESH,
            ))
        return copies

    for c in range(chunks):
        halving(0, c).start()

    pieces = ((cols, None), (all_cot, cot), (all_info, info))

    def across(d):
        to = lax.rem(way + d, ways)
        copies = []
        for i, (dst, src) in enumerate(pieces):
            if src is None:
                src = hidden.at[:, pl.ds(pl.multiple_of(to * width, width), width)]
            copies.append(pltpu.make_async_remote_copy(
                src_ref=src, dst_ref=dst.at[way],
                send_sem=f_send.at[d - 1, i], recv_sem=f_recv.at[d - 1, i],
                device_id={"fsdp": to}, device_id_type=pl.DeviceIdType.MESH,
            ))
        return copies

    for d in range(1, ways):
        for copy in across(d)[:2]:
            copy.start()
    own = []
    for i, (dst, src) in enumerate(pieces):
        if src is None:
            src = hidden.at[:, pl.ds(pl.multiple_of(way * width, width), width)]
        own.append(pltpu.make_async_copy(src, dst.at[way], local_sem.at[i]))
    for copy in own[:2]:
        copy.start()

    tile = 512

    def cut(i):
        return pl.ds(pl.multiple_of(i * tile, tile), tile)

    def norms():
        def add(i, total):
            block = hidden[:, cut(i)].astype(jnp.float32)
            block = block * block
            for lane in range(0, tile, HEAD):
                total = total + block[:, lane : lane + HEAD]
            return total

        squares = lax.fori_loop(
            0, hidden.shape[1] // tile, add, jnp.zeros((tok, HEAD), jnp.float32)
        )
        mean = jnp.sum(squares, axis=1, keepdims=True) / hidden.shape[1]
        info[0] = jnp.broadcast_to(lax.rsqrt(mean + norm_eps), (tok, HEAD))
        row = docs[...].astype(jnp.float32)
        info[1] = jnp.broadcast_to(row, (HEAD, tok)).T
        for d in range(1, ways):
            across(d)[2].start()
        own[2].start()

    def arrivals():
        for d in range(1, ways):
            for copy in across(d):
                copy.wait_recv()
        for copy in own:
            copy.wait()

    def find_angles():
        shape = (tok, HEAD)
        lane = lax.broadcasted_iota(jnp.int32, shape, 1)
        first_half = lane < HEAD // 2
        half_lane = jnp.where(first_half, lane, lane - HEAD // 2).astype(jnp.float32)
        frequency = jnp.exp(half_lane * (-2.0 * math.log(rope_base) / HEAD))
        token = lax.broadcasted_iota(jnp.int32, shape, 0).astype(jnp.float32)
        starts = []
        for s in range(DOCS):
            first = jnp.full((1, HEAD), float(far_index), jnp.float32)
            for f in range(ways):
                at = jnp.where(all_info[f, 1] == float(s), token + f * tok, float(far_index))
                first = jnp.minimum(first, jnp.min(at, axis=0, keepdims=True))
            starts.append(first)
        for f in range(ways):
            start = jnp.zeros(shape, jnp.float32)
            for s in range(DOCS):
                start = start + jnp.where(all_info[f, 1] == float(s), starts[s], 0.0)
            phases = (token + f * tok - start) * frequency
            sine = jnp.sin(phases)
            angles[f, 0] = jnp.cos(phases)
            angles[f, 1] = jnp.where(first_half, sine, -sine)

    def turn_back():
        for f in range(ways):
            back[pl.ds(f * tok, tok)] = turn(
                all_cot[f].astype(jnp.float32), angles[f, 0], angles[f, 1]
            ).astype(jnp.bfloat16)

    def activate(f):
        scale = all_info[f, 0][:, :1]

        def one(i, carry):
            normed = cols[f, :, cut(i)].astype(jnp.float32) * scale
            act[pl.ds(f * tok, tok), cut(i)] = (normed * gain[:, cut(i)]).astype(jnp.bfloat16)
            return carry

        lax.fori_loop(0, width // tile, one, 0)

    work = [arrivals, find_angles, turn_back]
    work += [functools.partial(activate, f) for f in range(ways)]

    def reduce_stage(k, c):
        part = pl.ds(c * step, step)
        halving(k, c).wait_recv()

        def total(m):
            mine = delta[m, bits[0], part] if k == 0 else kept[k][m, part]
            return mine.astype(jnp.float32) + recv[k][m, part].astype(jnp.float32)

        if k < stages - 1:
            count = islands >> (k + 2)
            following = orders[c][k + 1]
            below = 1 << sorted(orders[c][k + 1 :]).index(following)

            def place(j, bit):
                return j // below * (2 * below) + bit * below + j % below

            def to_send(j, carry):
                send[k + 1][j, part] = total(place(j, 1 - bits[following])).astype(jnp.bfloat16)
                return carry

            def to_keep(j, carry):
                kept[k + 1][j, part] = total(place(j, bits[following]))
                return carry

            lax.fori_loop(0, count, to_send, 0)
            halving(k + 1, c).start()
            lax.fori_loop(0, count, to_keep, 0)
        else:
            mean_delta = total(0) / islands
            fresh_mom = momentum_rate * mom[part] + mean_delta
            fresh = outer[part] - learn_rate * (mean_delta + momentum_rate * fresh_mom)
            weight[me, part] = fresh.astype(jnp.bfloat16)
            for copy in doubling(stages - 1, c):
                copy.start()
            new_mom[part] = fresh_mom
            new_outer[part] = fresh

    def gather_stage(k, c):
        for copy in doubling(k, c):
            copy.wait_recv()
        if k > 0:
            for copy in doubling(k - 1, c):
                copy.start()

    for tick in range(2 * stages + chunks - 1):
        for c in range(chunks):
            k = tick - c
            if 0 <= k < stages:
                reduce_stage(k, c)
                if tick == 1 and c == 0:
                    norms()
            elif stages <= k < 2 * stages:
                if work:
                    work.pop(0)()
                gather_stage(2 * stages - 1 - k, c)

    while work:
        work.pop(0)()

    def product(f):
        tokens = act[pl.ds(pl.multiple_of(f * tok, tok), tok), :]
        whole = weight[...].reshape(width, cot.shape[1])
        return jnp.dot(tokens, whole, preferred_element_type=jnp.float32)

    def swap(d):
        return pltpu.make_async_remote_copy(
            src_ref=part_out.at[d - 1], dst_ref=part_in.at[d - 1],
            send_sem=p_send.at[d - 1], recv_sem=p_recv.at[d - 1],
            device_id={"fsdp": lax.rem(way + d, ways)},
            device_id_type=pl.DeviceIdType.MESH,
        )

    for d in range(1, ways):
        part_out[d - 1] = product(lax.rem(way + d, ways)).astype(jnp.bfloat16)
        swap(d).start()
    projected = product(way)
    for c in range(chunks):
        for k in range(stages):
            halving(k, c).wait_send()
            for copy in doubling(k, c):
                copy.wait_send()
    for d in range(1, ways):
        for copy in across(d):
            copy.wait_send()
    for d in range(1, ways):
        swap(d).wait_recv()
        projected = projected + part_in[d - 1].astype(jnp.float32)
    keys[...] = turn(projected, angles[way, 0], -angles[way, 1]).astype(jnp.bfloat16)
    for d in range(1, ways):
        swap(d).wait_send()


def exchange(delta, outer, mom, hidden, cot, docs, gain):
    islands = lax.axis_size("island")
    ways = lax.axis_size("fsdp")
    stages = islands.bit_length() - 1
    rows, width = outer.shape
    chunks = CHUNKS if rows % (16 * CHUNKS) == 0 else 1
    tok, feats = hidden.shape
    bf, f32 = jnp.bfloat16, jnp.float32
    recv = [pltpu.VMEM((islands >> (k + 1), rows, width), bf) for k in range(stages)]
    send = [pltpu.VMEM((islands >> (k + 1), rows, width), bf) for k in range(1, stages)]
    kept = [pltpu.VMEM((islands >> (k + 1), rows, width), f32) for k in range(1, stages)]
    dma = pltpu.SemaphoreType.DMA
    vmem = pl.BlockSpec(memory_space=pltpu.VMEM)
    return pl.pallas_call(
        functools.partial(exchange_kernel, islands, ways, stages, chunks),
        out_shape=(
            jax.ShapeDtypeStruct((islands, rows, width), bf),
            jax.ShapeDtypeStruct((rows, width), f32),
            jax.ShapeDtypeStruct((rows, width), f32),
            jax.ShapeDtypeStruct((ways * tok, feats // ways), bf),
            jax.ShapeDtypeStruct((ways * tok, width), bf),
            jax.ShapeDtypeStruct((tok, width), bf),
        ),
        in_specs=[vmem] * 7,
        out_specs=[vmem] * 6,
        scratch_shapes=[
            pltpu.VMEM((ways, tok, feats // ways), bf),
            pltpu.VMEM((ways, tok, width), bf),
            pltpu.VMEM((2, tok, HEAD), f32),
            pltpu.VMEM((ways, 2, tok, HEAD), f32),
            pltpu.VMEM((max(ways - 1, 1), tok, width), bf),
            pltpu.VMEM((max(ways - 1, 1), tok, width), bf),
            pltpu.VMEM((ways, 2, tok, HEAD), f32),
        ] + recv + send + kept + [
            dma((stages, chunks)), dma((stages, chunks)),
            dma((chunks, islands)), dma((chunks, islands)),
            dma((max(ways - 1, 1), 3)), dma((max(ways - 1, 1), 3)), dma((3,)),
            dma((max(ways - 1, 1),)), dma((max(ways - 1, 1),)),
        ],
        compiler_params=pltpu.CompilerParams(
            collective_id=0, has_side_effects=True, vmem_limit_bytes=56 * 1024 * 1024
        ),
    )(delta.reshape(islands // 2, 2, rows, width), outer, mom, hidden, cot, docs, gain)


def body(hidden, gain, doc_ids, cotangent, pseudo_grad, outer_weight, momentum):
    gain_row = gain.astype(jnp.float32)[None, :]
    weight, new_outer, new_momentum, act, back, keys = exchange(
        pseudo_grad[0], outer_weight, momentum, hidden[0], cotangent[0], doc_ids, gain_row
    )
    weight = weight.reshape(-1, weight.shape[2])
    grad_weight = lax.dot_general(
        act, back, (((0,), (0,)), ((), ())), preferred_element_type=jnp.float32
    ).astype(jnp.bfloat16)
    hidden_grad = lax.dot_general(
        back, weight, (((1,), (1,)), ((), ())), preferred_element_type=jnp.float32
    )
    grad_gain = jnp.sum(hidden_grad * act.astype(jnp.float32), axis=0, keepdims=True) / gain_row
    return keys[None], grad_weight[None], grad_gain, new_outer, new_momentum


def solution(mesh):
    placed = (
        P("island", "fsdp", None),
        P("fsdp"),
        P("island", "fsdp"),
        P("island", "fsdp", None),
        P("island", "fsdp", None),
        P(("fsdp", "island"), None),
        P(("fsdp", "island"), None),
    )
    return jax.shard_map(
        body,
        mesh=mesh,
        in_specs=placed,
        out_specs=(
            P("island", "fsdp", None),
            P("island", "fsdp", None),
            P("island", "fsdp"),
            P(("fsdp", "island"), None),
            P(("fsdp", "island"), None),
        ),
        check_vma=False,
    )
```

```python
import functools
import math

import jax
import jax.numpy as jnp
from jax import lax
from jax.experimental import pallas as pl
from jax.experimental.pallas import tpu as pltpu
from jax.sharding import PartitionSpec as P

HEAD = 128
DOCS = 8


learn_rate = 0.7
momentum_rate = 0.9
norm_eps = 1e-05
rope_base = 500000.0
far_index = 1 << 30


def turn(values, cosine, sine):
    heads = [values[:, i : i + HEAD] for i in range(0, values.shape[1], HEAD)]
    return jnp.concatenate(
        [head * cosine + pltpu.roll(head, HEAD // 2, 1) * sine for head in heads], axis=1
    )


CHUNKS = 4


def orders_for(stages, chunk):
    return list(range(stages))


def exchange_kernel(islands, ways, stages, chunks, *refs):
    (delta, outer, mom, hidden, cot, docs, gain) = refs[:7]
    (weight, new_outer, new_mom, act, back, keys) = refs[7:13]
    (cols, all_cot, info, all_info, part_out, part_in, angles) = refs[13:20]
    scratch = list(refs[20:])
    recv = [scratch.pop(0) for _ in range(stages)]
    send = [None] + [scratch.pop(0) for _ in range(stages - 1)]
    kept = [None] + [scratch.pop(0) for _ in range(stages - 1)]
    rs_send, rs_recv, ag_send, ag_recv, f_send, f_recv, local_sem, p_send, p_recv = scratch
    tok = cot.shape[0]

    me = lax.axis_index("island")
    way = lax.axis_index("fsdp")
    bits = [me // (1 << k) % 2 for k in range(stages)]
    partners = [me + (1 - 2 * bits[k]) * (1 << k) for k in range(stages)]
    rows = outer.shape[0]
    step = rows // chunks
    width = hidden.shape[1] // ways

    barrier = pltpu.get_barrier_semaphore()
    for k in range(stages):
        pl.semaphore_signal(
            barrier, inc=1, device_id={"island": partners[k]},
            device_id_type=pl.DeviceIdType.MESH,
        )
    for d in range(1, ways):
        pl.semaphore_signal(
            barrier, inc=1, device_id={"fsdp": lax.rem(way + d, ways)},
            device_id_type=pl.DeviceIdType.MESH,
        )
    pl.semaphore_wait(barrier, stages + ways - 1)

    orders = [orders_for(stages, c) for c in range(chunks)]

    def halving(k, c):
        part = pl.ds(c * step, step)
        bit = orders[c][k]
        src = delta.at[:, 1 - bits[0], part] if k == 0 else send[k].at[:, part]
        return pltpu.make_async_remote_copy(
            src_ref=src, dst_ref=recv[k].at[:, part],
            send_sem=rs_send.at[k, c], recv_sem=rs_recv.at[k, c],
            device_id={"island": partners[bit]}, device_id_type=pl.DeviceIdType.MESH,
        )

    def doubling(k, c):
        part = pl.ds(c * step, step)
        bit = orders[c][k]
        fixed = sum(bits[b] * (1 << b) for b in orders[c][: k + 1])
        copies = []
        for j in range(islands >> (k + 1)):
            slot = islands - islands // (1 << k) + j
            block = fixed + sum((j >> i & 1) << b for i, b in enumerate(orders[c][k + 1 :]))
            copies.append(pltpu.make_async_remote_copy(
                src_ref=weight.at[block, part], dst_ref=weight.at[block, part],
                send_sem=ag_send.at[c, slot], recv_sem=ag_recv.at[c, slot],
                device_id={"island": partners[bit]}, device_id_type=pl.DeviceIdType.MESH,
            ))
        return copies

    for c in range(chunks):
        halving(0, c).start()

    pieces = ((cols, None), (all_cot, cot), (all_info, info))

    def across(d):
        to = lax.rem(way + d, ways)
        copies = []
        for i, (dst, src) in enumerate(pieces):
            if src is None:
                src = hidden.at[:, pl.ds(pl.multiple_of(to * width, width), width)]
            copies.append(pltpu.make_async_remote_copy(
                src_ref=src, dst_ref=dst.at[way],
                send_sem=f_send.at[d - 1, i], recv_sem=f_recv.at[d - 1, i],
                device_id={"fsdp": to}, device_id_type=pl.DeviceIdType.MESH,
            ))
        return copies

    for d in range(1, ways):
        for copy in across(d)[:2]:
            copy.start()
    own = []
    for i, (dst, src) in enumerate(pieces):
        if src is None:
            src = hidden.at[:, pl.ds(pl.multiple_of(way * width, width), width)]
        own.append(pltpu.make_async_copy(src, dst.at[way], local_sem.at[i]))
    for copy in own[:2]:
        copy.start()

    tile = 512

    def cut(i):
        return pl.ds(pl.multiple_of(i * tile, tile), tile)

    def norms():
        def add(i, total):
            block = hidden[:, cut(i)].astype(jnp.float32)
            block = block * block
            for lane in range(0, tile, HEAD):
                total = total + block[:, lane : lane + HEAD]
            return total

        squares = lax.fori_loop(
            0, hidden.shape[1] // tile, add, jnp.zeros((tok, HEAD), jnp.float32)
        )
        mean = jnp.sum(squares, axis=1, keepdims=True) / hidden.shape[1]
        info[0] = jnp.broadcast_to(lax.rsqrt(mean + norm_eps), (tok, HEAD))
        row = docs[...].astype(jnp.float32)
        info[1] = jnp.broadcast_to(row, (HEAD, tok)).T
        for d in range(1, ways):
            across(d)[2].start()
        own[2].start()

    def arrivals():
        for d in range(1, ways):
            for copy in across(d):
                copy.wait_recv()
        for copy in own:
            copy.wait()

    def find_angles():
        shape = (tok, HEAD)
        lane = lax.broadcasted_iota(jnp.int32, shape, 1)
        first_half = lane < HEAD // 2
        half_lane = jnp.where(first_half, lane, lane - HEAD // 2).astype(jnp.float32)
        frequency = jnp.exp(half_lane * (-2.0 * math.log(rope_base) / HEAD))
        token = lax.broadcasted_iota(jnp.int32, shape, 0).astype(jnp.float32)
        starts = []
        for s in range(DOCS):
            first = jnp.full((1, HEAD), float(far_index), jnp.float32)
            for f in range(ways):
                at = jnp.where(all_info[f, 1] == float(s), token + f * tok, float(far_index))
                first = jnp.minimum(first, jnp.min(at, axis=0, keepdims=True))
            starts.append(first)
        for f in range(ways):
            start = jnp.zeros(shape, jnp.float32)
            for s in range(DOCS):
                start = start + jnp.where(all_info[f, 1] == float(s), starts[s], 0.0)
            phases = (token + f * tok - start) * frequency
            sine = jnp.sin(phases)
            angles[f, 0] = jnp.cos(phases)
            angles[f, 1] = jnp.where(first_half, sine, -sine)

    def turn_back():
        for f in range(ways):
            back[pl.ds(f * tok, tok)] = turn(
                all_cot[f].astype(jnp.float32), angles[f, 0], angles[f, 1]
            ).astype(jnp.bfloat16)

    def activate(f):
        scale = all_info[f, 0][:, :1]

        def one(i, carry):
            normed = cols[f, :, cut(i)].astype(jnp.float32) * scale
            act[pl.ds(f * tok, tok), cut(i)] = (normed * gain[:, cut(i)]).astype(jnp.bfloat16)
            return carry

        lax.fori_loop(0, width // tile, one, 0)

    work = [arrivals, find_angles, turn_back]
    work += [functools.partial(activate, f) for f in range(ways)]

    def reduce_stage(k, c):
        part = pl.ds(c * step, step)
        halving(k, c).wait_recv()

        def total(m):
            mine = delta[m, bits[0], part] if k == 0 else kept[k][m, part]
            return mine.astype(jnp.float32) + recv[k][m, part].astype(jnp.float32)

        if k < stages - 1:
            count = islands >> (k + 2)
            following = orders[c][k + 1]
            below = 1 << sorted(orders[c][k + 1 :]).index(following)

            def place(j, bit):
                return j // below * (2 * below) + bit * below + j % below

            def to_send(j, carry):
                send[k + 1][j, part] = total(place(j, 1 - bits[following])).astype(jnp.bfloat16)
                return carry

            def to_keep(j, carry):
                kept[k + 1][j, part] = total(place(j, bits[following]))
                return carry

            lax.fori_loop(0, count, to_send, 0)
            halving(k + 1, c).start()
            lax.fori_loop(0, count, to_keep, 0)
        else:
            mean_delta = total(0) / islands
            fresh_mom = momentum_rate * mom[part] + mean_delta
            fresh = outer[part] - learn_rate * (mean_delta + momentum_rate * fresh_mom)
            weight[me, part] = fresh.astype(jnp.bfloat16)
            for copy in doubling(stages - 1, c):
                copy.start()
            new_mom[part] = fresh_mom
            new_outer[part] = fresh

    def gather_stage(k, c):
        for copy in doubling(k, c):
            copy.wait_recv()
        if k > 0:
            for copy in doubling(k - 1, c):
                copy.start()

    for tick in range(2 * stages + chunks - 1):
        for c in range(chunks):
            k = tick - c
            if 0 <= k < stages:
                reduce_stage(k, c)
                if tick == 1 and c == 0:
                    norms()
            elif stages <= k < 2 * stages:
                gather_stage(2 * stages - 1 - k, c)
                if work and 2 * stages - 1 - k <= 2:
                    work.pop(0)()

    while work:
        work.pop(0)()

    def product(f):
        tokens = act[pl.ds(pl.multiple_of(f * tok, tok), tok), :]
        whole = weight[...].reshape(width, cot.shape[1])
        return jnp.dot(tokens, whole, preferred_element_type=jnp.float32)

    def swap(d):
        return pltpu.make_async_remote_copy(
            src_ref=part_out.at[d - 1], dst_ref=part_in.at[d - 1],
            send_sem=p_send.at[d - 1], recv_sem=p_recv.at[d - 1],
            device_id={"fsdp": lax.rem(way + d, ways)},
            device_id_type=pl.DeviceIdType.MESH,
        )

    for d in range(1, ways):
        part_out[d - 1] = product(lax.rem(way + d, ways)).astype(jnp.bfloat16)
        swap(d).start()
    projected = product(way)
    for c in range(chunks):
        for k in range(stages):
            halving(k, c).wait_send()
            for copy in doubling(k, c):
                copy.wait_send()
    for d in range(1, ways):
        for copy in across(d):
            copy.wait_send()
    for d in range(1, ways):
        swap(d).wait_recv()
        projected = projected + part_in[d - 1].astype(jnp.float32)
    keys[...] = turn(projected, angles[way, 0], -angles[way, 1]).astype(jnp.bfloat16)
    for d in range(1, ways):
        swap(d).wait_send()


def exchange(delta, outer, mom, hidden, cot, docs, gain):
    islands = lax.axis_size("island")
    ways = lax.axis_size("fsdp")
    stages = islands.bit_length() - 1
    rows, width = outer.shape
    chunks = CHUNKS if rows % (16 * CHUNKS) == 0 else 1
    tok, feats = hidden.shape
    bf, f32 = jnp.bfloat16, jnp.float32
    recv = [pltpu.VMEM((islands >> (k + 1), rows, width), bf) for k in range(stages)]
    send = [pltpu.VMEM((islands >> (k + 1), rows, width), bf) for k in range(1, stages)]
    kept = [pltpu.VMEM((islands >> (k + 1), rows, width), f32) for k in range(1, stages)]
    dma = pltpu.SemaphoreType.DMA
    vmem = pl.BlockSpec(memory_space=pltpu.VMEM)
    return pl.pallas_call(
        functools.partial(exchange_kernel, islands, ways, stages, chunks),
        out_shape=(
            jax.ShapeDtypeStruct((islands, rows, width), bf),
            jax.ShapeDtypeStruct((rows, width), f32),
            jax.ShapeDtypeStruct((rows, width), f32),
            jax.ShapeDtypeStruct((ways * tok, feats // ways), bf),
            jax.ShapeDtypeStruct((ways * tok, width), bf),
            jax.ShapeDtypeStruct((tok, width), bf),
        ),
        in_specs=[vmem] * 7,
        out_specs=[vmem] * 6,
        scratch_shapes=[
            pltpu.VMEM((ways, tok, feats // ways), bf),
            pltpu.VMEM((ways, tok, width), bf),
            pltpu.VMEM((2, tok, HEAD), f32),
            pltpu.VMEM((ways, 2, tok, HEAD), f32),
            pltpu.VMEM((max(ways - 1, 1), tok, width), bf),
            pltpu.VMEM((max(ways - 1, 1), tok, width), bf),
            pltpu.VMEM((ways, 2, tok, HEAD), f32),
        ] + recv + send + kept + [
            dma((stages, chunks)), dma((stages, chunks)),
            dma((chunks, islands)), dma((chunks, islands)),
            dma((max(ways - 1, 1), 3)), dma((max(ways - 1, 1), 3)), dma((3,)),
            dma((max(ways - 1, 1),)), dma((max(ways - 1, 1),)),
        ],
        compiler_params=pltpu.CompilerParams(
            collective_id=0, has_side_effects=True, vmem_limit_bytes=56 * 1024 * 1024
        ),
    )(delta.reshape(islands // 2, 2, rows, width), outer, mom, hidden, cot, docs, gain)


def body(hidden, gain, doc_ids, cotangent, pseudo_grad, outer_weight, momentum):
    gain_row = gain.astype(jnp.float32)[None, :]
    weight, new_outer, new_momentum, act, back, keys = exchange(
        pseudo_grad[0], outer_weight, momentum, hidden[0], cotangent[0], doc_ids, gain_row
    )
    weight = weight.reshape(-1, weight.shape[2])
    grad_weight = lax.dot_general(
        act, back, (((0,), (0,)), ((), ())), preferred_element_type=jnp.float32
    ).astype(jnp.bfloat16)
    hidden_grad = lax.dot_general(
        back, weight, (((1,), (1,)), ((), ())), preferred_element_type=jnp.float32
    )
    grad_gain = jnp.sum(hidden_grad * act.astype(jnp.float32), axis=0, keepdims=True) / gain_row
    return keys[None], grad_weight[None], grad_gain, new_outer, new_momentum


def solution(mesh):
    placed = (
        P("island", "fsdp", None),
        P("fsdp"),
        P("island", "fsdp"),
        P("island", "fsdp", None),
        P("island", "fsdp", None),
        P(("fsdp", "island"), None),
        P(("fsdp", "island"), None),
    )
    return jax.shard_map(
        body,
        mesh=mesh,
        in_specs=placed,
        out_specs=(
            P("island", "fsdp", None),
            P("island", "fsdp", None),
            P("island", "fsdp"),
            P(("fsdp", "island"), None),
            P(("fsdp", "island"), None),
        ),
        check_vma=False,
    )
```
